128 devices in a mesh: col: 128 (over z, x, y, core).
Axes of the slice: x: 4, y: 4, z: 4, core: 2. Of those that a mesh axis runs over, the one named last changes fastest.
Arguments:
- covariance: float32 [2, 8192, 8192], P(None, 'col'), may hold values from -6 to 6, as said below
- forcing: float32 [2, 8192, 8192], P(None, 'col'), may hold values from -24 to 24, as said below
- coefficient: float32 [2, 64, 128], replicated, may hold values from 0.5 to 1.5
- y_operator: float32 [2, 64, 64], replicated, may hold values from -0.75 to 0.75
- z_operator: float32 [2, 128, 128], replicated, may hold values from -0.5 to 0.5
Outputs:
- advanced: float32 [2, 8192, 8192], P(None, 'col')
The draws below stay inside these ranges and needn't reach their ends.
Inputs may be any that keep to these rules, and one draw needn't show every extreme that they name: Each harmonic's covariance is symmetric. Each harmonic's forcing is symmetric.
All inputs are finite; a program needn't handle non-finite values.
Results may differ from the reference program's by a relative error of at most 0.0001.
Values sent between devices are 32-bit elements; how exact they have to be, the bound alone decides.
A program may use at most 192 MiB of HBM per device.

```python
import jax
import jax.numpy as jnp
from jax import lax

NY = 64
NZ = 128
N = 8192


def symmetric_draw(key, scale):
    raw = jax.random.normal(key, (2, N, N), jnp.float32)
    sym = jnp.clip((raw + jnp.swapaxes(raw, 1, 2)) * 0.70710678, -6.0, 6.0)
    return scale * sym


def draw_covariance(key, part):
    return symmetric_draw(jax.random.fold_in(key, 11), 1.0)


def draw_forcing(key, part):
    return symmetric_draw(jax.random.fold_in(key, 23), 4.0)


def gaussian(rng, shape, spread, most, kind=jnp.bfloat16):
    drawn = spread * jax.random.normal(rng, shape, jnp.float32)
    return jnp.clip(drawn, min=-most, max=most).astype(kind)


def setup_inputs(seed: int = 0) -> dict:
    splits = jax.random.split(jax.random.key(seed), 6)
    covariance = draw_covariance(jax.random.fold_in(splits[5], 71), 0)
    forcing = draw_forcing(jax.random.fold_in(splits[5], 71), 0)
    coefficient = jnp.clip(jax.random.uniform(splits[2], (2, NY, NZ), jnp.float32, 0.5, 1.5), 0.5, 1.5)
    y_operator = gaussian(splits[3], (2, NY, NY), NY ** -0.5, 0.75, jnp.float32)
    z_operator = gaussian(splits[4], (2, NZ, NZ), NZ ** -0.5, 0.5, jnp.float32)
    return {"covariance": covariance, "forcing": forcing, "coefficient": coefficient, "y_operator": y_operator, "z_operator": z_operator}


step_size = 0.2


def combined(values, y_matrix, z_matrix):
    along_y = jnp.einsum("ya,azc->yzc", y_matrix, values, precision=lax.Precision.HIGHEST)
    along_z = jnp.einsum("zb,ybc->yzc", z_matrix, values, precision=lax.Precision.HIGHEST)
    return along_y + along_z


def apply_operator(columns, y_matrix, z_matrix, gain_field):
    grid = columns.reshape(NY, NZ, -1)
    inner = gain_field[:, :, None] * combined(grid, y_matrix, z_matrix)
    return combined(inner, y_matrix, z_matrix).reshape(NY * NZ, -1)


def slope_of(state, y_matrix, z_matrix, gain_field, source):
    product = apply_operator(state, y_matrix, z_matrix, gain_field)
    return product + product.T + source


def reference(covariance, forcing, coefficient, y_operator, z_operator):
    results = []
    for harmonic in range(2):
        start = covariance[harmonic]
        args = (y_operator[harmonic], z_operator[harmonic], coefficient[harmonic], forcing[harmonic])
        slope_one = slope_of(start, *args)
        slope_two = slope_of(start + (0.5 * step_size) * slope_one, *args)
        slope_three = slope_of(start + (0.5 * step_size) * slope_two, *args)
        slope_four = slope_of(start + step_size * slope_three, *args)
        results.append(start + (step_size / 6.0) * (slope_one + 2.0 * slope_two + 2.0 * slope_three + slope_four))
    return jnp.stack(results)
```

```python
import functools

import jax
import jax.numpy as jnp
from jax import lax
from jax.experimental import pallas as pl
from jax.experimental.pallas import tpu as pltpu
from jax.sharding import PartitionSpec as P

MESH = pl.DeviceIdType.MESH

step_size = 0.2

LINES = 64
WIDTH = 128
ROWS = 64
SLAB = LINES * ROWS
DEVICES = 128


def split(values):
    high = values.astype(jnp.bfloat16)
    low = (values - high.astype(jnp.float32)).astype(jnp.bfloat16)
    return high, low


def kernel(
    covariance, forcing, coefficient, y_tiled, z_operator, advanced,
    held_c, held_g, held_w, held_p, inner, along_y, outbox, inbox, y_factor, z_factor,
    load_sem, store_sem, send_sem, recv_sem,
):
    me = lax.axis_index("col")
    chip = me // 2
    place_z, place_x, place_y = chip // 16, (chip // 4) % 4, chip % 4

    barrier = pltpu.get_barrier_semaphore()

    def greet(step, carry):
        pl.semaphore_signal(
            barrier, inc=1, device_id=(lax.rem(me + step, DEVICES),), device_id_type=MESH
        )
        return carry

    lax.fori_loop(1, DEVICES, greet, 0)

    def load(source, target, sem, h):
        def line(y, carry):
            pltpu.make_async_copy(
                source.at[h, :, pl.ds(pl.multiple_of(y * WIDTH, WIDTH), WIDTH)],
                target.at[h, pl.ds(pl.multiple_of(y * ROWS, ROWS), ROWS), :],
                sem,
            ).start()
            return carry

        lax.fori_loop(0, LINES, line, 0)

    def wait_load(target, sem, h):
        pltpu.make_async_copy(target.at[h], target.at[h], sem).wait()

    for h in range(2):
        load(covariance, held_c, load_sem.at[0, h], h)
    for h in range(2):
        load(forcing, held_g, load_sem.at[1, h], h)

    lane = lax.broadcasted_iota(jnp.int32, (32, WIDTH), 1)
    left_half = lane < 64

    for h in range(2):
        tiled = y_tiled[h]
        high, low = split(tiled)
        first = lax.broadcasted_iota(jnp.int32, tiled.shape, 1) < 128
        y_factor[h] = jnp.where(first, high.astype(jnp.float32), low.astype(jnp.float32)).astype(
            jnp.bfloat16
        )
        high, low = split(z_operator[h].T)
        z_factor[h, 0:128, 0:128] = high
        z_factor[h, 0:128, 128:256] = low
        z_factor[h, 128:256, 0:128] = high
        z_factor[h, 128:256, 128:256] = jnp.zeros_like(low)

    def contract_y(source, h):
        factor = y_factor[h]

        def pair(j, carry):
            row = j * 2
            both = jnp.concatenate(
                [source[pl.ds(row + k, LINES, stride=ROWS), :] for k in range(2)], axis=1
            )
            high, low = split(both)
            stacked = jnp.concatenate([high, low, high, low], axis=0)
            out = jnp.dot(factor, stacked, preferred_element_type=jnp.float32)
            for k in range(2):
                along_y[pl.ds(row + k, LINES, stride=ROWS), :] = out[:, k * 128 : (k + 1) * 128]
            return carry

        lax.fori_loop(0, ROWS // 2, pair, 0, unroll=4)

    def combined(source, h, y):
        rows = pl.ds(pl.multiple_of(y * ROWS, ROWS), ROWS)
        high, low = split(source[rows, :])
        out = jnp.dot(
            jnp.concatenate([high, low], axis=1), z_factor[h], preferred_element_type=jnp.float32
        )
        return out[:, 0:128] + out[:, 128:256] + along_y[rows, :]

    def first_half(source, h):
        contract_y(source, h)

        def line(y, carry):
            gain = step_size * coefficient[h, pl.ds(y, 1), :]
            inner[pl.ds(pl.multiple_of(y * ROWS, ROWS), ROWS), :] = gain * combined(source, h, y)
            return carry

        lax.fori_loop(0, LINES, line, 0, unroll=4)
        contract_y(inner, h)

    def target_line(q):
        u, v, w = q % 4, (q // 4) % 4, q // 16
        return (
            ((place_z + u) % 4) * 16 + ((place_x + u + v) % 4) * 4 + (place_y + u + v + w) % 4
        )

    def post(exchange, h, lines, values):
        turned = jnp.concatenate(values, axis=0).T
        for core in range(2):
            upper = turned[core * 64 : core * 64 + 32]
            lower = turned[core * 64 + 32 : core * 64 + 64]
            blocks = (
                jnp.where(left_half, upper, pltpu.roll(lower, 64, 1)),
                jnp.where(left_half, pltpu.roll(upper, 64, 1), lower),
            )
            for k in range(2):
                device = lines[k] * 2 + core
                outbox[h, device] = blocks[k]

                @pl.when(device == me)
                def _():
                    inbox[exchange, h, device] = blocks[k]

                @pl.when(device != me)
                def _():
                    pltpu.make_async_remote_copy(
                        src_ref=outbox.at[h, device],
                        dst_ref=inbox.at[exchange, h, me],
                        send_sem=send_sem.at[exchange, h],
                        recv_sem=recv_sem.at[exchange, h],
                        device_id=(device,),
                        device_id_type=MESH,
                    ).start()

    def post_all(exchange, h, value_of):
        def pair(s, carry):
            lines = [target_line(2 * s), target_line(2 * s + 1)]
            post(exchange, h, lines, [value_of(y) for y in lines])
            return carry

        lax.fori_loop(0, LINES // 2, pair, 0)

    def everything(exchange, h):
        whole = inbox.at[exchange, h, pl.ds(0, DEVICES - 1)]
        return pltpu.make_async_remote_copy(
            src_ref=whole,
            dst_ref=whole,
            send_sem=send_sem.at[exchange, h],
            recv_sem=recv_sem.at[exchange, h],
            device_id=(lax.rem(me + 1, DEVICES),),
            device_id_type=MESH,
        )

    def arrived(exchange, h, y):
        zero, one = inbox[exchange, h, 2 * y], inbox[exchange, h, 2 * y + 1]
        return jnp.concatenate(
            [
                jnp.where(left_half, zero, pltpu.roll(one, 64, 1)),
                jnp.where(left_half, pltpu.roll(zero, 64, 1), one),
            ],
            axis=0,
        )

    def rows_of(y):
        return pl.ds(pl.multiple_of(y * ROWS, ROWS), ROWS)

    def stage_zero(h, carry):
        wait_load(held_c, load_sem.at[0, h], h)
        first_half(held_c.at[h], h)

        @pl.when(h == 0)
        def _():
            pl.semaphore_wait(barrier, DEVICES - 1)

        def value_of(y):
            value = combined(inner, h, y)
            held_w[h, rows_of(y), :] = value
            return value

        post_all(0, h, value_of)
        return carry

    lax.fori_loop(0, 2, stage_zero, 0)

    def stage_one(h, carry):
        wait_load(held_g, load_sem.at[1, h], h)
        everything(0, h).wait()

        def gather(y, carry):
            rows = rows_of(y)
            held_g[h, rows, :] = (
                step_size * held_g[h, rows, :] + held_w[h, rows, :] + arrived(0, h, y)
            )
            return carry

        lax.fori_loop(0, LINES, gather, 0, unroll=2)
        first_half(held_g.at[h], h)

        def line(y, carry):
            held_w[h, rows_of(y), :] = combined(inner, h, y)
            return carry

        lax.fori_loop(0, LINES, line, 0, unroll=4)
        first_half(held_w.at[h], h)

        def value_of(y):
            rows = rows_of(y)
            second = combined(inner, h, y)
            held_p[h, rows, :] = second
            return second + (4.0 / 3.0) * held_w[h, rows, :]

        post_all(1, h, value_of)
        return carry

    lax.fori_loop(0, 2, stage_one, 0)

    def stage_between(h, carry):
        first_half(held_p.at[h], h)

        def line(y, carry):
            rows = rows_of(y)
            third = combined(inner, h, y) * (1.0 / 24.0)
            one = held_w[h, rows, :]
            held_c[h, rows, :] = (
                held_c[h, rows, :]
                + held_g[h, rows, :]
                + 0.5 * one
                + (1.0 / 6.0) * held_p[h, rows, :]
                + third
            )
            held_w[h, rows, :] = (5.0 / 18.0) * one + third
            return carry

        lax.fori_loop(0, LINES, line, 0, unroll=2)
        return carry

    lax.fori_loop(0, 2, stage_between, 0)

    def stage_two(h, carry):
        everything(1, h).wait()

        def gather(y, carry):
            held_p[h, rows_of(y), :] = arrived(1, h, y)
            return carry

        lax.fori_loop(0, LINES, gather, 0, unroll=2)
        first_half(held_p.at[h], h)

        def value_of(y):
            rows = rows_of(y)
            eighth = 0.125 * combined(inner, h, y)
            held_c[h, rows, :] = held_c[h, rows, :] + (1.0 / 6.0) * held_p[h, rows, :] + eighth
            return held_w[h, rows, :] + eighth

        post_all(2, h, value_of)
        return carry

    lax.fori_loop(0, 2, stage_two, 0)

    def stage_last(h, carry):
        everything(2, h).wait()

        def line(y, carry):
            rows = rows_of(y)
            held_g[h, rows, :] = held_c[h, rows, :] + arrived(2, h, y)
            pltpu.make_async_copy(
                held_g.at[h, rows, :],
                advanced.at[h, :, pl.ds(pl.multiple_of(y * WIDTH, WIDTH), WIDTH)],
                store_sem.at[h],
            ).start()
            return carry

        lax.fori_loop(0, LINES, line, 0, unroll=2)
        return carry

    lax.fori_loop(0, 2, stage_last, 0)
    for h in range(2):
        wait_load(held_g, store_sem.at[h], h)


def on_device(covariance, forcing, coefficient, y_operator, z_operator):
    slab = pltpu.VMEM((2, SLAB, WIDTH), jnp.float32)
    part = pltpu.VMEM((SLAB, WIDTH), jnp.float32)
    hbm = pl.BlockSpec(memory_space=pl.ANY)
    vmem = pl.BlockSpec(memory_space=pltpu.VMEM)
    return pl.pallas_call(
        kernel,
        out_shape=jax.ShapeDtypeStruct(covariance.shape, jnp.float32),
        in_specs=[hbm, hbm, vmem, vmem, vmem],
        out_specs=hbm,
        scratch_shapes=[
            slab, slab, slab, slab, part, part,
            pltpu.VMEM((2, DEVICES, 32, WIDTH), jnp.float32),
            pltpu.VMEM((3, 2, DEVICES, 32, WIDTH), jnp.float32),
            pltpu.VMEM((2, LINES, 256), jnp.bfloat16),
            pltpu.VMEM((2, 256, 256), jnp.bfloat16),
            pltpu.SemaphoreType.DMA((2, 2)),
            pltpu.SemaphoreType.DMA((2,)),
            pltpu.SemaphoreType.DMA((3, 2)),
            pltpu.SemaphoreType.DMA((3, 2)),
        ],
        compiler_params=pltpu.CompilerParams(
            collective_id=0, has_side_effects=True, vmem_limit_bytes=56 * 2**20
        ),
        cost_estimate=pl.CostEstimate(
            flops=25 * 10**9, bytes_accessed=12 * 2**20, transcendentals=0
        ),
    )(covariance, forcing, coefficient, jnp.tile(y_operator, (1, 1, 4)), z_operator)


def solution(mesh):
    placed = (P(None, "col", None), P(None, "col", None), P(), P(), P())
    return jax.shard_map(
        on_device, mesh=mesh, in_specs=placed, out_specs=P(None, "col", None), check_vma=False
    )
```

```python
import functools

import jax
import jax.numpy as jnp
from jax import lax
from jax.experimental import pallas as pl
from jax.experimental.pallas import tpu as pltpu
from jax.sharding import PartitionSpec as P

MESH = pl.DeviceIdType.MESH

step_size = 0.2

LINES = 64
WIDTH = 128
ROWS = 64
SLAB = LINES * ROWS
DEVICES = 128


def split(values):
    high = values.astype(jnp.bfloat16)
    low = (values - high.astype(jnp.float32)).astype(jnp.bfloat16)
    return high, low


def kernel(
    covariance, forcing, coefficient, y_operator, z_operator, advanced,
    held_c, held_g, held_w, held_p, inner, outer, along_y, outbox, inbox, y_factor, z_factor,
    load_sem, store_sem, send_sem, recv_sem,
):
    me = lax.axis_index("col")
    chip = me // 2
    place_z, place_x, place_y = chip // 16, (chip // 4) % 4, chip % 4

    barrier = pltpu.get_barrier_semaphore()

    def greet(step, carry):
        pl.semaphore_signal(
            barrier, inc=1, device_id=(lax.rem(me + step, DEVICES),), device_id_type=MESH
        )
        return carry

    lax.fori_loop(1, DEVICES, greet, 0)

    def load(source, target, sem, h):
        def line(y, carry):
            pltpu.make_async_copy(
                source.at[h, :, pl.ds(pl.multiple_of(y * WIDTH, WIDTH), WIDTH)],
                target.at[h, pl.ds(pl.multiple_of(y * ROWS, ROWS), ROWS), :],
                sem,
            ).start()
            return carry

        lax.fori_loop(0, LINES, line, 0)

    def wait_load(target, sem, h):
        pltpu.make_async_copy(target.at[h], target.at[h], sem).wait()

    for h in range(2):
        load(covariance, held_c, load_sem.at[0, h], h)
    for h in range(2):
        load(forcing, held_g, load_sem.at[1, h], h)

    def rows_of(y):
        return pl.ds(pl.multiple_of(y * ROWS, ROWS), ROWS)

    lane = lax.broadcasted_iota(jnp.int32, (32, WIDTH), 1)
    left_half = lane < 64

    for h in range(2):
        high, low = split(y_operator[h])
        pieces = [half.astype(jnp.float32) for half in (high, high, low, low)]
        y_factor[h] = jnp.concatenate(pieces, axis=1).astype(jnp.bfloat16)
        high, low = split(z_operator[h].T)
        z_factor[h, 0:128, 0:128] = high
        z_factor[h, 0:128, 128:256] = low
        z_factor[h, 128:256, 0:128] = high
        z_factor[h, 128:256, 128:256] = jnp.zeros_like(low)

    def contract_y(source, h):
        group = 16
        factor = y_factor[h]

        def step(j, carry):
            row = j * group
            both = jnp.concatenate(
                [source[pl.ds(row + k, LINES, stride=ROWS), :] for k in range(group)], axis=1
            )
            high, low = split(both)
            stacked = jnp.concatenate([high, low, high, low], axis=0)
            out = jnp.dot(factor, stacked, preferred_element_type=jnp.float32)
            for k in range(group):
                along_y[pl.ds(row + k, LINES, stride=ROWS), :] = out[:, k * 128 : (k + 1) * 128]
            return carry

        lax.fori_loop(0, ROWS // group, step, 0, unroll=2)

    def combined(source, h, write):
        group = 32

        def step(j, carry):
            rows = pl.ds(pl.multiple_of(j * (group * ROWS), group * ROWS), group * ROWS)
            high, low = split(source[rows, :])
            out = jnp.dot(
                jnp.concatenate([high, low], axis=1),
                z_factor[h],
                preferred_element_type=jnp.float32,
            )
            value = out[:, 0:128] + out[:, 128:256] + along_y[rows, :]
            for k in range(group):
                write(j * group + k, value[k * ROWS : (k + 1) * ROWS])
            return carry

        lax.fori_loop(0, LINES // group, step, 0)

    def first_half(source, h):
        contract_y(source, h)

        def write(y, value):
            inner[rows_of(y), :] = (step_size * coefficient[h, pl.ds(y, 1), :]) * value

        combined(source, h, write)
        contract_y(inner, h)

    def target_line(q):
        u, v, w = q % 4, (q // 4) % 4, q // 16
        return (
            ((place_z + u) % 4) * 16 + ((place_x + u + v) % 4) * 4 + (place_y + u + v + w) % 4
        )

    def post(exchange, h, source):
        group = 8

        def step(s, carry):
            lines = [target_line(s * group + k) for k in range(group)]
            for k in range(0, group, 2):
                pair = [source[rows_of(y), :] for y in lines[k : k + 2]]
                turned = jnp.concatenate(pair, axis=0).T
                for core in range(2):
                    upper = turned[core * 64 : core * 64 + 32]
                    lower = turned[core * 64 + 32 : core * 64 + 64]
                    outbox[h, lines[k] * 2 + core] = jnp.where(
                        left_half, upper, pltpu.roll(lower, 64, 1)
                    )
                    outbox[h, lines[k + 1] * 2 + core] = jnp.where(
                        left_half, pltpu.roll(upper, 64, 1), lower
                    )

            def send(device):
                pltpu.make_async_remote_copy(
                    src_ref=outbox.at[h, device],
                    dst_ref=inbox.at[exchange, h, me],
                    send_sem=send_sem.at[exchange, h],
                    recv_sem=recv_sem.at[exchange, h],
                    device_id=(device,),
                    device_id_type=MESH,
                ).start()

            for k in range(group):
                if k > 0:
                    for core in range(2):
                        send(lines[k] * 2 + core)
                else:

                    @pl.when(s > 0)
                    def _():
                        for core in range(2):
                            send(lines[0] * 2 + core)

                    @pl.when(s == 0)
                    def _():
                        send(me + 1 - 2 * lax.rem(me, 2))

            return carry

        lax.fori_loop(0, LINES // group, step, 0)
        inbox[exchange, h, me] = outbox[h, me]

    def everything(exchange, h):
        whole = inbox.at[exchange, h, pl.ds(0, DEVICES - 1)]
        return pltpu.make_async_remote_copy(
            src_ref=whole,
            dst_ref=whole,
            send_sem=send_sem.at[exchange, h],
            recv_sem=recv_sem.at[exchange, h],
            device_id=(lax.rem(me + 1, DEVICES),),
            device_id_type=MESH,
        )

    def arrived(exchange, h, y):
        zero, one = inbox[exchange, h, 2 * y], inbox[exchange, h, 2 * y + 1]
        return jnp.concatenate(
            [
                jnp.where(left_half, zero, pltpu.roll(one, 64, 1)),
                jnp.where(left_half, pltpu.roll(zero, 64, 1), one),
            ],
            axis=0,
        )

    def stage_zero(h):
        wait_load(held_c, load_sem.at[0, h], h)
        first_half(held_c.at[h], h)

        def write(y, value):
            held_w[h, rows_of(y), :] = value

        combined(inner, h, write)
        if h == 0:
            pl.semaphore_wait(barrier, DEVICES - 1)
        post(0, h, held_w.at[h])

    def stage_one(h):
        wait_load(held_g, load_sem.at[1, h], h)
        everything(0, h).wait()

        def gather(y, carry):
            rows = rows_of(y)
            held_g[h, rows, :] = (
                step_size * held_g[h, rows, :] + held_w[h, rows, :] + arrived(0, h, y)
            )
            return carry

        lax.fori_loop(0, LINES, gather, 0, unroll=8)
        first_half(held_g.at[h], h)

        def write_one(y, value):
            held_w[h, rows_of(y), :] = value

        combined(inner, h, write_one)
        first_half(held_w.at[h], h)

        def write_two(y, value):
            held_p[h, rows_of(y), :] = value
            outer[rows_of(y), :] = value + (4.0 / 3.0) * held_w[h, rows_of(y), :]

        combined(inner, h, write_two)
        post(1, h, outer)

    def stage_between(h):
        first_half(held_p.at[h], h)

        def write(y, value):
            rows = rows_of(y)
            third = value * (1.0 / 24.0)
            one = held_w[h, rows, :]
            held_c[h, rows, :] = (
                held_c[h, rows, :]
                + held_g[h, rows, :]
                + 0.5 * one
                + (1.0 / 6.0) * held_p[h, rows, :]
                + third
            )
            held_w[h, rows, :] = (5.0 / 18.0) * one + third

        combined(inner, h, write)

    def stage_two(h):
        everything(1, h).wait()

        def gather(y, carry):
            held_p[h, rows_of(y), :] = arrived(1, h, y)
            return carry

        lax.fori_loop(0, LINES, gather, 0, unroll=8)
        first_half(held_p.at[h], h)

        def write(y, value):
            rows = rows_of(y)
            eighth = 0.125 * value
            held_c[h, rows, :] = held_c[h, rows, :] + (1.0 / 6.0) * held_p[h, rows, :] + eighth
            outer[rows, :] = held_w[h, rows, :] + eighth

        combined(inner, h, write)
        post(2, h, outer)

    def stage_last(h):
        everything(2, h).wait()

        def group(g, carry):
            for k in range(8):
                rows = rows_of(g * 8 + k)
                held_g[h, rows, :] = held_c[h, rows, :] + arrived(2, h, g * 8 + k)
            for k in range(8):
                y = g * 8 + k
                pltpu.make_async_copy(
                    held_g.at[h, rows_of(y), :],
                    advanced.at[h, :, pl.ds(pl.multiple_of(y * WIDTH, WIDTH), WIDTH)],
                    store_sem.at[h],
                ).start()
            return carry

        lax.fori_loop(0, LINES // 8, group, 0)

    for stage in (stage_zero, stage_one, stage_between, stage_two, stage_last):
        for h in range(2):
            stage(h)
    for h in range(2):
        wait_load(held_g, store_sem.at[h], h)


def on_device(covariance, forcing, coefficient, y_operator, z_operator):
    slab = pltpu.VMEM((2, SLAB, WIDTH), jnp.float32)
    part = pltpu.VMEM((SLAB, WIDTH), jnp.float32)
    hbm = pl.BlockSpec(memory_space=pl.ANY)
    vmem = pl.BlockSpec(memory_space=pltpu.VMEM)
    return pl.pallas_call(
        kernel,
        out_shape=jax.ShapeDtypeStruct(covariance.shape, jnp.float32),
        in_specs=[hbm, hbm, vmem, vmem, vmem],
        out_specs=hbm,
        scratch_shapes=[
            slab, slab, slab, slab, part, part, part,
            pltpu.VMEM((2, DEVICES, 32, WIDTH), jnp.float32),
            pltpu.VMEM((3, 2, DEVICES, 32, WIDTH), jnp.float32),
            pltpu.VMEM((2, LINES, 256), jnp.bfloat16),
            pltpu.VMEM((2, 256, 256), jnp.bfloat16),
            pltpu.SemaphoreType.DMA((2, 2)),
            pltpu.SemaphoreType.DMA((2,)),
            pltpu.SemaphoreType.DMA((3, 2)),
            pltpu.SemaphoreType.DMA((3, 2)),
        ],
        compiler_params=pltpu.CompilerParams(
            collective_id=0, has_side_effects=True, vmem_limit_bytes=56 * 2**20
        ),
        cost_estimate=pl.CostEstimate(
            flops=25 * 10**9, bytes_accessed=12 * 2**20, transcendentals=0
        ),
    )(covariance, forcing, coefficient, y_operator, z_operator)


def solution(mesh):
    placed = (P(None, "col", None), P(None, "col", None), P(), P(), P())
    return jax.shard_map(
        on_device, mesh=mesh, in_specs=placed, out_specs=P(None, "col", None), check_vma=False
    )
```

```python
import functools

import jax
import jax.numpy as jnp
from jax import lax
from jax.experimental import pallas as pl
from jax.experimental.pallas import tpu as pltpu
from jax.sharding import PartitionSpec as P

MESH = pl.DeviceIdType.MESH

step_size = 0.2

LINES = 64
WIDTH = 128
ROWS = 64
SLAB = LINES * ROWS
DEVICES = 128
AHEAD_ONE = 7
AHEAD_TWO = 6


def split(values):
    high = values.astype(jnp.bfloat16)
    low = (values - high.astype(jnp.float32)).astype(jnp.bfloat16)
    return high, low


def kernel(
    covariance, forcing, coefficient, y_operator, z_operator, advanced,
    held_c, held_g, held_w, held_p, inner, outer, along_y, outbox, inbox, y_factor, z_factor,
    load_sem, store_sem, send_sem, recv_sem,
):
    me = lax.axis_index("col")
    chip = me // 2
    place_z, place_x, place_y = chip // 16, (chip // 4) % 4, chip % 4
    turn = 1 + 2 * lax.rem(me, 2)

    barrier = pltpu.get_barrier_semaphore()

    def greet(step, carry):
        pl.semaphore_signal(
            barrier, inc=1, device_id=(lax.rem(me + step, DEVICES),), device_id_type=MESH
        )
        return carry

    lax.fori_loop(1, DEVICES, greet, 0)

    def load(source, target, sem, h):
        def line(y, carry):
            pltpu.make_async_copy(
                source.at[h, :, pl.ds(pl.multiple_of(y * WIDTH, WIDTH), WIDTH)],
                target.at[h, pl.ds(pl.multiple_of(y * ROWS, ROWS), ROWS), :],
                sem,
            ).start()
            return carry

        lax.fori_loop(0, LINES, line, 0)

    def wait_load(target, sem, h):
        pltpu.make_async_copy(target.at[h], target.at[h], sem).wait()

    for h in range(2):
        load(covariance, held_c, load_sem.at[0, h], h)
    for h in range(2):
        load(forcing, held_g, load_sem.at[1, h], h)

    def rows_of(y):
        return pl.ds(pl.multiple_of(y * ROWS, ROWS), ROWS)

    lane = lax.broadcasted_iota(jnp.int32, (32, WIDTH), 1)
    left_half = lane < 64

    for h in range(2):
        high, low = split(y_operator[h])
        pieces = [half.astype(jnp.float32) for half in (high, high, low, low)]
        y_factor[h] = jnp.concatenate(pieces, axis=1).astype(jnp.bfloat16)
        high, low = split(z_operator[h].T)
        z_factor[h, 0:128, 0:128] = high
        z_factor[h, 0:128, 128:256] = low
        z_factor[h, 128:256, 0:128] = high
        z_factor[h, 128:256, 128:256] = jnp.zeros_like(low)

    def contract_y(source, h):
        group = 16
        factor = y_factor[h]

        def step(j, carry):
            row = j * group
            both = jnp.concatenate(
                [source[pl.ds(row + k, LINES, stride=ROWS), :] for k in range(group)], axis=1
            )
            high, low = split(both)
            stacked = jnp.concatenate([high, low, high, low], axis=0)
            out = jnp.dot(factor, stacked, preferred_element_type=jnp.float32)
            for k in range(group):
                along_y[pl.ds(row + k, LINES, stride=ROWS), :] = out[:, k * 128 : (k + 1) * 128]
            return carry

        lax.fori_loop(0, ROWS // group, step, 0, unroll=2)

    def combined(source, h, write):
        group = 32

        def step(j, carry):
            rows = pl.ds(pl.multiple_of(j * (group * ROWS), group * ROWS), group * ROWS)
            high, low = split(source[rows, :])
            out = jnp.dot(
                jnp.concatenate([high, low], axis=1),
                z_factor[h],
                preferred_element_type=jnp.float32,
            )
            value = out[:, 0:128] + out[:, 128:256] + along_y[rows, :]
            for k in range(group):
                write(j * group + k, value[k * ROWS : (k + 1) * ROWS])
            return carry

        lax.fori_loop(0, LINES // group, step, 0)

    def first_half(source, h):
        contract_y(source, h)

        def write(y, value):
            inner[rows_of(y), :] = (step_size * coefficient[h, pl.ds(y, 1), :]) * value

        combined(source, h, write)
        contract_y(inner, h)

    def target_line(q):
        u, v, w = turn * (q % 4), turn * ((q // 4) % 4), turn * (q // 16)
        return (
            ((place_z + u) % 4) * 16
            + ((place_x + 2 * u + v) % 4) * 4
            + (place_y + u + v + w) % 4
        )

    def post(exchange, h, source):
        group = 8
        box = exchange % 2

        def step(s, carry):
            lines = [target_line(s * group + k) for k in range(group)]
            for k in range(0, group, 2):
                pair = [source[rows_of(y), :] for y in lines[k : k + 2]]
                turned = jnp.concatenate(pair, axis=0).T
                for core in range(2):
                    upper = turned[core * 64 : core * 64 + 32]
                    lower = turned[core * 64 + 32 : core * 64 + 64]
                    outbox[box, h, lines[k] * 2 + core] = jnp.where(
                        left_half, upper, pltpu.roll(lower, 64, 1)
                    )
                    outbox[box, h, lines[k + 1] * 2 + core] = jnp.where(
                        left_half, pltpu.roll(upper, 64, 1), lower
                    )

            def send(device):
                pltpu.make_async_remote_copy(
                    src_ref=outbox.at[box, h, device],
                    dst_ref=inbox.at[exchange, h, me],
                    send_sem=send_sem.at[exchange, h, s],
                    recv_sem=recv_sem.at[exchange, h],
                    device_id=(device,),
                    device_id_type=MESH,
                ).start()

            for k in range(group):
                if k > 0:
                    for core in range(2):
                        send(lines[k] * 2 + core)
                else:

                    @pl.when(s > 0)
                    def _():
                        for core in range(2):
                            send(lines[0] * 2 + core)

                    @pl.when(s == 0)
                    def _():
                        send(me + 1 - 2 * lax.rem(me, 2))

            return carry

        lax.fori_loop(0, LINES // group, step, 0)
        inbox[exchange, h, me] = outbox[box, h, me]

    def moved(exchange, h, group, blocks):
        part = inbox.at[exchange, h, pl.ds(0, blocks)]
        return pltpu.make_async_remote_copy(
            src_ref=part,
            dst_ref=part,
            send_sem=send_sem.at[exchange, h, group],
            recv_sem=recv_sem.at[exchange, h],
            device_id=(lax.rem(me + 1, DEVICES),),
            device_id_type=MESH,
        )

    def wait_sent(exchange, h, first, last):
        for group in range(first, last):
            moved(exchange, h, group, 16 if group else 15).wait_send()

    def wait_arrived(exchange, h):
        moved(exchange, h, 0, DEVICES - 1).wait_recv()

    def arrived(exchange, h, y):
        zero, one = inbox[exchange, h, 2 * y], inbox[exchange, h, 2 * y + 1]
        return jnp.concatenate(
            [
                jnp.where(left_half, zero, pltpu.roll(one, 64, 1)),
                jnp.where(left_half, pltpu.roll(zero, 64, 1), one),
            ],
            axis=0,
        )

    def stage_zero(h):
        wait_load(held_c, load_sem.at[0, h], h)
        first_half(held_c.at[h], h)

        def write(y, value):
            held_w[h, rows_of(y), :] = value

        combined(inner, h, write)
        if h == 0:
            pl.semaphore_wait(barrier, DEVICES - 1)
        post(0, h, held_w.at[h])

    def stage_one(h):
        wait_load(held_g, load_sem.at[1, h], h)

        def start(g, carry):
            rows = pl.ds(pl.multiple_of(g * 512, 512), 512)
            held_g[h, rows, :] = step_size * held_g[h, rows, :] + held_w[h, rows, :]
            return carry

        lax.fori_loop(0, SLAB // 512, start, 0)
        first_half(held_g.at[h], h)

        def write(y, value):
            held_p[h, rows_of(y), :] = value

        combined(inner, h, write)
        if h == 0:
            post(1, h, held_p.at[h])

    def stage_two(h):
        wait_sent(0, h, 0, 8)
        wait_arrived(0, h)

        def gather(y, carry):
            rows = rows_of(y)
            value = arrived(0, h, y)
            held_w[h, rows, :] = value
            held_c[h, rows, :] = held_c[h, rows, :] + held_g[h, rows, :] + value
            return carry

        lax.fori_loop(0, LINES, gather, 0, unroll=8)
        first_half(held_w.at[h], h)

        def write(y, value):
            rows = rows_of(y)
            held_g[h, rows, :] = (
                (1.0 / 6.0) * value
                + (1.0 / 24.0) * held_p[h, rows, :]
                + (1.0 / 3.0) * held_w[h, rows, :]
            )

        combined(inner, h, write)

    def stage_three(h):
        wait_arrived(1, h)
        wait_sent(1, h, AHEAD_ONE if h == 0 else AHEAD_TWO, 8)

        def gather(y, carry):
            rows = rows_of(y)
            value = arrived(1, h, y)
            held_g[h, rows, :] = held_g[h, rows, :] + 0.125 * value
            held_w[h, rows, :] = 0.5 * held_w[h, rows, :] + (1.0 / 6.0) * (
                held_p[h, rows, :] + value
            )
            return carry

        lax.fori_loop(0, LINES, gather, 0, unroll=8)
        first_half(held_g.at[h], h)

        def write_one(y, value):
            rows = rows_of(y)
            held_w[h, rows, :] = held_w[h, rows, :] + value

        combined(inner, h, write_one)
        first_half(held_w.at[h], h)

        def write_two(y, value):
            rows = rows_of(y)
            total = value + 0.5 * held_p[h, rows, :]
            outer[rows, :] = total
            held_c[h, rows, :] = held_c[h, rows, :] + total

        combined(inner, h, write_two)
        if h == 0:
            wait_sent(1, 1, 0, AHEAD_TWO)
        post(2, h, outer)

    def stage_last(h):
        wait_arrived(2, h)
        wait_sent(2, h, 0, 8)

        def group(g, carry):
            for k in range(8):
                rows = rows_of(g * 8 + k)
                held_g[h, rows, :] = held_c[h, rows, :] + arrived(2, h, g * 8 + k)
            for k in range(8):
                y = g * 8 + k
                pltpu.make_async_copy(
                    held_g.at[h, rows_of(y), :],
                    advanced.at[h, :, pl.ds(pl.multiple_of(y * WIDTH, WIDTH), WIDTH)],
                    store_sem.at[h],
                ).start()
            return carry

        lax.fori_loop(0, LINES // 8, group, 0)

    for stage in (stage_zero, stage_one, stage_two):
        for h in range(2):
            stage(h)
    wait_sent(1, 0, 0, AHEAD_ONE)
    post(1, 1, held_p.at[1])
    for stage in (stage_three, stage_last):
        for h in range(2):
            stage(h)
    for h in range(2):
        wait_load(held_g, store_sem.at[h], h)


def on_device(covariance, forcing, coefficient, y_operator, z_operator):
    slab = pltpu.VMEM((2, SLAB, WIDTH), jnp.float32)
    part = pltpu.VMEM((SLAB, WIDTH), jnp.float32)
    hbm = pl.BlockSpec(memory_space=pl.ANY)
    vmem = pl.BlockSpec(memory_space=pltpu.VMEM)
    return pl.pallas_call(
        kernel,
        out_shape=jax.ShapeDtypeStruct(covariance.shape, jnp.float32),
        in_specs=[hbm, hbm, vmem, vmem, vmem],
        out_specs=hbm,
        scratch_shapes=[
            slab, slab, slab, slab, part, part, part,
            pltpu.VMEM((2, 2, DEVICES, 32, WIDTH), jnp.float32),
            pltpu.VMEM((3, 2, DEVICES, 32, WIDTH), jnp.float32),
            pltpu.VMEM((2, LINES, 256), jnp.bfloat16),
            pltpu.VMEM((2, 256, 256), jnp.bfloat16),
            pltpu.SemaphoreType.DMA((2, 2)),
            pltpu.SemaphoreType.DMA((2,)),
            pltpu.SemaphoreType.DMA((3, 2, 8)),
            pltpu.SemaphoreType.DMA((3, 2)),
        ],
        compiler_params=pltpu.CompilerParams(
            collective_id=0, has_side_effects=True, vmem_limit_bytes=56 * 2**20
        ),
        cost_estimate=pl.CostEstimate(
            flops=25 * 10**9, bytes_accessed=12 * 2**20, transcendentals=0
        ),
    )(covariance, forcing, coefficient, y_operator, z_operator)


def solution(mesh):
    placed = (P(None, "col", None), P(None, "col", None), P(), P(), P())
    return jax.shard_map(
        on_device, mesh=mesh, in_specs=placed, out_specs=P(None, "col", None), check_vma=False
    )
```

```python
import functools

import jax
import jax.numpy as jnp
from jax import lax
from jax.experimental import pallas as pl
from jax.experimental.pallas import tpu as pltpu
from jax.sharding import PartitionSpec as P

MESH = pl.DeviceIdType.MESH

step_size = 0.2

LINES = 64
WIDTH = 128
ROWS = 64
SLAB = LINES * ROWS
DEVICES = 128
AHEAD_ONE = 7
AHEAD_TWO = 6


def split(values):
    high = values.astype(jnp.bfloat16)
    low = (values - high.astype(jnp.float32)).astype(jnp.bfloat16)
    return high, low


def kernel(
    covariance, forcing, coefficient, y_operator, z_operator, advanced,
    held_c, held_g, held_w, held_p, inner, outer, along_y, outbox, inbox, y_factor, z_factor,
    load_sem, store_sem, send_sem, recv_sem,
):
    me = lax.axis_index("col")
    chip = me // 2
    place_z, place_x, place_y = chip // 16, (chip // 4) % 4, chip % 4
    turn = 1 + 2 * lax.rem(me, 2)

    barrier = pltpu.get_barrier_semaphore()

    def load(source, target, sem, h):
        def line(y, carry):
            pltpu.make_async_copy(
                source.at[h, :, pl.ds(pl.multiple_of(y * WIDTH, WIDTH), WIDTH)],
                target.at[h, pl.ds(pl.multiple_of(y * ROWS, ROWS), ROWS), :],
                sem,
            ).start()
            return carry

        lax.fori_loop(0, LINES, line, 0)

    def wait_load(target, sem, h):
        pltpu.make_async_copy(target.at[h], target.at[h], sem).wait()

    load(covariance, held_c, load_sem.at[0, 0], 0)

    def greet(step, carry):
        pl.semaphore_signal(
            barrier, inc=1, device_id=(lax.rem(me + step, DEVICES),), device_id_type=MESH
        )
        return carry

    lax.fori_loop(1, DEVICES, greet, 0)

    def rows_of(y):
        return pl.ds(pl.multiple_of(y * ROWS, ROWS), ROWS)

    lane = lax.broadcasted_iota(jnp.int32, (32, WIDTH), 1)
    left_half = lane < 64

    for h in range(2):
        high, low = split(y_operator[h])
        pieces = [half.astype(jnp.float32) for half in (high, high, low, low)]
        y_factor[h] = jnp.concatenate(pieces, axis=1).astype(jnp.bfloat16)
        high, low = split(z_operator[h].T)
        z_factor[h, 0:128, 0:128] = high
        z_factor[h, 0:128, 128:256] = low
        z_factor[h, 128:256, 0:128] = high
        z_factor[h, 128:256, 128:256] = jnp.zeros_like(low)

    def contract_y(source, h):
        group = 16
        factor = y_factor[h]

        def step(j, carry):
            row = j * group
            both = jnp.concatenate(
                [source[pl.ds(row + k, LINES, stride=ROWS), :] for k in range(group)], axis=1
            )
            high, low = split(both)
            stacked = jnp.concatenate([high, low, high, low], axis=0)
            out = jnp.dot(factor, stacked, preferred_element_type=jnp.float32)
            for k in range(group):
                along_y[pl.ds(row + k, LINES, stride=ROWS), :] = out[:, k * 128 : (k + 1) * 128]
            return carry

        lax.fori_loop(0, ROWS // group, step, 0, unroll=2)

    def combined(source, h, write):
        group = 32

        def step(j, carry):
            rows = pl.ds(pl.multiple_of(j * (group * ROWS), group * ROWS), group * ROWS)
            high, low = split(source[rows, :])
            out = jnp.dot(
                jnp.concatenate([high, low], axis=1),
                z_factor[h],
                preferred_element_type=jnp.float32,
            )
            value = out[:, 0:128] + out[:, 128:256] + along_y[rows, :]
            for k in range(group):
                write(j * group + k, value[k * ROWS : (k + 1) * ROWS])
            return carry

        lax.fori_loop(0, LINES // group, step, 0)

    def first_half(source, h):
        contract_y(source, h)

        def write(y, value):
            inner[rows_of(y), :] = (step_size * coefficient[h, pl.ds(y, 1), :]) * value

        combined(source, h, write)
        contract_y(inner, h)

    def target_line(q):
        u, v, w = turn * (q % 4), turn * ((q // 4) % 4), turn * (q // 16)
        return (
            ((place_z + u) % 4) * 16
            + ((place_x + 2 * u + v) % 4) * 4
            + (place_y + u + v + w) % 4
        )

    def post(exchange, h, source):
        group = 8
        box = exchange % 2

        def step(s, carry):
            lines = [target_line(s * group + k) for k in range(group)]
            for k in range(0, group, 2):
                pair = [source[rows_of(y), :] for y in lines[k : k + 2]]
                turned = jnp.concatenate(pair, axis=0).T
                for core in range(2):
                    upper = turned[core * 64 : core * 64 + 32]
                    lower = turned[core * 64 + 32 : core * 64 + 64]
                    outbox[box, h, lines[k] * 2 + core] = jnp.where(
                        left_half, upper, pltpu.roll(lower, 64, 1)
                    )
                    outbox[box, h, lines[k + 1] * 2 + core] = jnp.where(
                        left_half, pltpu.roll(upper, 64, 1), lower
                    )

            def send(device):
                pltpu.make_async_remote_copy(
                    src_ref=outbox.at[box, h, device],
                    dst_ref=inbox.at[exchange, h, me],
                    send_sem=send_sem.at[exchange, h, s],
                    recv_sem=recv_sem.at[exchange, h],
                    device_id=(device,),
                    device_id_type=MESH,
                ).start()

            for k in range(group):
                if k > 0:
                    for core in range(2):
                        send(lines[k] * 2 + core)
                else:

                    @pl.when(s > 0)
                    def _():
                        for core in range(2):
                            send(lines[0] * 2 + core)

                    @pl.when(s == 0)
                    def _():
                        send(me + 1 - 2 * lax.rem(me, 2))

            return carry

        lax.fori_loop(0, LINES // group, step, 0)
        inbox[exchange, h, me] = outbox[box, h, me]

    def moved(exchange, h, group, blocks):
        part = inbox.at[exchange, h, pl.ds(0, blocks)]
        return pltpu.make_async_remote_copy(
            src_ref=part,
            dst_ref=part,
            send_sem=send_sem.at[exchange, h, group],
            recv_sem=recv_sem.at[exchange, h],
            device_id=(lax.rem(me + 1, DEVICES),),
            device_id_type=MESH,
        )

    def wait_sent(exchange, h, first, last):
        for group in range(first, last):
            moved(exchange, h, group, 16 if group else 15).wait_send()

    def wait_arrived(exchange, h):
        moved(exchange, h, 0, DEVICES - 1).wait_recv()

    def arrived(exchange, h, y):
        zero, one = inbox[exchange, h, 2 * y], inbox[exchange, h, 2 * y + 1]
        return jnp.concatenate(
            [
                jnp.where(left_half, zero, pltpu.roll(one, 64, 1)),
                jnp.where(left_half, pltpu.roll(zero, 64, 1), one),
            ],
            axis=0,
        )

    def stage_zero(h):
        wait_load(held_c, load_sem.at[0, h], h)
        first_half(held_c.at[h], h)

        def write(y, value):
            held_w[h, rows_of(y), :] = value

        combined(inner, h, write)
        if h == 0:
            pl.semaphore_wait(barrier, DEVICES - 1)
        post(0, h, held_w.at[h])

    def stage_one(h):
        wait_load(held_g, load_sem.at[1, h], h)

        def start(g, carry):
            rows = pl.ds(pl.multiple_of(g * 512, 512), 512)
            held_g[h, rows, :] = step_size * held_g[h, rows, :] + held_w[h, rows, :]
            return carry

        lax.fori_loop(0, SLAB // 512, start, 0)
        first_half(held_g.at[h], h)

        def write(y, value):
            held_p[h, rows_of(y), :] = value

        combined(inner, h, write)
        if h == 0:
            post(1, h, held_p.at[h])

    def stage_two(h):
        wait_sent(0, h, 0, 8)
        wait_arrived(0, h)

        def gather(y, carry):
            rows = rows_of(y)
            value = arrived(0, h, y)
            held_w[h, rows, :] = value
            held_c[h, rows, :] = held_c[h, rows, :] + held_g[h, rows, :] + value
            return carry

        lax.fori_loop(0, LINES, gather, 0, unroll=8)
        first_half(held_w.at[h], h)

        def write(y, value):
            rows = rows_of(y)
            held_g[h, rows, :] = (
                (1.0 / 6.0) * value
                + (1.0 / 24.0) * held_p[h, rows, :]
                + (1.0 / 3.0) * held_w[h, rows, :]
            )

        combined(inner, h, write)

    def stage_three(h):
        wait_arrived(1, h)
        wait_sent(1, h, AHEAD_ONE if h == 0 else AHEAD_TWO, 8)

        def gather(y, carry):
            rows = rows_of(y)
            value = arrived(1, h, y)
            held_g[h, rows, :] = held_g[h, rows, :] + 0.125 * value
            held_w[h, rows, :] = 0.5 * held_w[h, rows, :] + (1.0 / 6.0) * (
                held_p[h, rows, :] + value
            )
            return carry

        lax.fori_loop(0, LINES, gather, 0, unroll=8)
        first_half(held_g.at[h], h)

        def write_one(y, value):
            rows = rows_of(y)
            held_w[h, rows, :] = held_w[h, rows, :] + value

        combined(inner, h, write_one)
        first_half(held_w.at[h], h)

        def write_two(y, value):
            rows = rows_of(y)
            total = value + 0.5 * held_p[h, rows, :]
            outer[rows, :] = total
            held_c[h, rows, :] = held_c[h, rows, :] + total

        combined(inner, h, write_two)
        if h == 0:
            wait_sent(1, 1, 0, AHEAD_TWO)
        post(2, h, outer)

    def stage_last(h):
        wait_arrived(2, h)
        wait_sent(2, h, 0, 8)

        def group(g, carry):
            for k in range(8):
                rows = rows_of(g * 8 + k)
                held_g[h, rows, :] = held_c[h, rows, :] + arrived(2, h, g * 8 + k)
            for k in range(8):
                y = g * 8 + k
                pltpu.make_async_copy(
                    held_g.at[h, rows_of(y), :],
                    advanced.at[h, :, pl.ds(pl.multiple_of(y * WIDTH, WIDTH), WIDTH)],
                    store_sem.at[h],
                ).start()
            return carry

        lax.fori_loop(0, LINES // 8, group, 0)

    stage_zero(0)
    load(covariance, held_c, load_sem.at[0, 1], 1)
    for h in range(2):
        load(forcing, held_g, load_sem.at[1, h], h)
    stage_zero(1)
    for stage in (stage_one, stage_two):
        for h in range(2):
            stage(h)
    wait_sent(1, 0, 0, AHEAD_ONE)
    post(1, 1, held_p.at[1])
    for stage in (stage_three, stage_last):
        for h in range(2):
            stage(h)
    for h in range(2):
        wait_load(held_g, store_sem.at[h], h)


def on_device(covariance, forcing, coefficient, y_operator, z_operator):
    slab = pltpu.VMEM((2, SLAB, WIDTH), jnp.float32)
    part = pltpu.VMEM((SLAB, WIDTH), jnp.float32)
    hbm = pl.BlockSpec(memory_space=pl.ANY)
    vmem = pl.BlockSpec(memory_space=pltpu.VMEM)
    return pl.pallas_call(
        kernel,
        out_shape=jax.ShapeDtypeStruct(covariance.shape, jnp.float32),
        in_specs=[hbm, hbm, vmem, vmem, vmem],
        out_specs=hbm,
        scratch_shapes=[
            slab, slab, slab, slab, part, part, part,
            pltpu.VMEM((2, 2, DEVICES, 32, WIDTH), jnp.float32),
            pltpu.VMEM((3, 2, DEVICES, 32, WIDTH), jnp.float32),
            pltpu.VMEM((2, LINES, 256), jnp.bfloat16),
            pltpu.VMEM((2, 256, 256), jnp.bfloat16),
            pltpu.SemaphoreType.DMA((2, 2)),
            pltpu.SemaphoreType.DMA((2,)),
            pltpu.SemaphoreType.DMA((3, 2, 8)),
            pltpu.SemaphoreType.DMA((3, 2)),
        ],
        compiler_params=pltpu.CompilerParams(
            collective_id=0, has_side_effects=True, vmem_limit_bytes=56 * 2**20
        ),
        cost_estimate=pl.CostEstimate(
            flops=25 * 10**9, bytes_accessed=12 * 2**20, transcendentals=0
        ),
    )(covariance, forcing, coefficient, y_operator, z_operator)


def solution(mesh):
    placed = (P(None, "col", None), P(None, "col", None), P(), P(), P())
    return jax.shard_map(
        on_device, mesh=mesh, in_specs=placed, out_specs=P(None, "col", None), check_vma=False
    )
```

```python
import functools

import jax
import jax.numpy as jnp
from jax import lax
from jax.experimental import pallas as pl
from jax.experimental.pallas import tpu as pltpu
from jax.sharding import PartitionSpec as P

MESH = pl.DeviceIdType.MESH

step_size = 0.2

LINES = 64
WIDTH = 128
ROWS = 64
SLAB = LINES * ROWS
DEVICES = 128
AHEAD_ONE = 7
AHEAD_TWO = 6


def split(values):
    high = values.astype(jnp.bfloat16)
    low = (values - high.astype(jnp.float32)).astype(jnp.bfloat16)
    return high, low


def kernel(
    covariance, forcing, coefficient, y_operator, z_operator, advanced,
    held_c, held_g, held_w, held_p, inner, outer, along_y, outbox, inbox, y_factor, z_factor,
    load_sem, store_sem, send_sem, recv_sem,
):
    me = lax.axis_index("col")
    chip = me // 2
    place_z, place_x, place_y = chip // 16, (chip // 4) % 4, chip % 4
    turn = 1 + 2 * lax.rem(me, 2)

    barrier = pltpu.get_barrier_semaphore()

    def load(source, target, sem, h):
        def line(y, carry):
            pltpu.make_async_copy(
                source.at[h, :, pl.ds(pl.multiple_of(y * WIDTH, WIDTH), WIDTH)],
                target.at[h, pl.ds(pl.multiple_of(y * ROWS, ROWS), ROWS), :],
                sem,
            ).start()
            return carry

        lax.fori_loop(0, LINES, line, 0)

    def wait_load(target, sem, h):
        pltpu.make_async_copy(target.at[h], target.at[h], sem).wait()

    load(covariance, held_c, load_sem.at[0, 0], 0)

    def greet(step, carry):
        pl.semaphore_signal(
            barrier, inc=1, device_id=(lax.rem(me + step, DEVICES),), device_id_type=MESH
        )
        return carry

    lax.fori_loop(1, DEVICES, greet, 0)

    def rows_of(y):
        return pl.ds(pl.multiple_of(y * ROWS, ROWS), ROWS)

    lane = lax.broadcasted_iota(jnp.int32, (32, WIDTH), 1)
    left_half = lane < 64

    def prepare(h):
        high, low = split(y_operator[h])
        pieces = [half.astype(jnp.float32) for half in (high, high, low, low)]
        y_factor[h] = jnp.concatenate(pieces, axis=1).astype(jnp.bfloat16)
        high, low = split(z_operator[h].T)
        z_factor[h, 0:128, 0:128] = high
        z_factor[h, 0:128, 128:256] = low
        z_factor[h, 128:256, 0:128] = high
        z_factor[h, 128:256, 128:256] = jnp.zeros_like(low)

    def contract_y(source, h):
        group = 16
        factor = y_factor[h]

        def step(j, carry):
            row = j * group
            both = jnp.concatenate(
                [source[pl.ds(row + k, LINES, stride=ROWS), :] for k in range(group)], axis=1
            )
            high, low = split(both)
            stacked = jnp.concatenate([high, low, high, low], axis=0)
            out = jnp.dot(factor, stacked, preferred_element_type=jnp.float32)
            for k in range(group):
                along_y[pl.ds(row + k, LINES, stride=ROWS), :] = out[:, k * 128 : (k + 1) * 128]
            return carry

        lax.fori_loop(0, ROWS // group, step, 0, unroll=4)

    def combined(source, h, write):
        group = 32

        def step(j, carry):
            rows = pl.ds(pl.multiple_of(j * (group * ROWS), group * ROWS), group * ROWS)
            high, low = split(source[rows, :])
            out = jnp.dot(
                jnp.concatenate([high, low], axis=1),
                z_factor[h],
                preferred_element_type=jnp.float32,
            )
            value = out[:, 0:128] + out[:, 128:256] + along_y[rows, :]
            for k in range(group):
                write(j * group + k, value[k * ROWS : (k + 1) * ROWS])
            return carry

        lax.fori_loop(0, LINES // group, step, 0)

    def first_half(source, h):
        contract_y(source, h)

        def write(y, value):
            inner[rows_of(y), :] = (step_size * coefficient[h, pl.ds(y, 1), :]) * value

        combined(source, h, write)
        contract_y(inner, h)

    def target_line(q):
        u, v, w = turn * (q % 4), turn * ((q // 4) % 4), turn * (q // 16)
        return (
            ((place_z + u) % 4) * 16
            + ((place_x + 2 * u + v) % 4) * 4
            + (place_y + u + v + w) % 4
        )

    def post(exchange, h, source):
        group = 8
        box = exchange % 2

        def step(s, carry):
            lines = [target_line(s * group + k) for k in range(group)]
            for k in range(0, group, 2):
                pair = [source[rows_of(y), :] for y in lines[k : k + 2]]
                turned = jnp.concatenate(pair, axis=0).T
                for core in range(2):
                    upper = turned[core * 64 : core * 64 + 32]
                    lower = turned[core * 64 + 32 : core * 64 + 64]
                    outbox[box, h, lines[k] * 2 + core] = jnp.where(
                        left_half, upper, pltpu.roll(lower, 64, 1)
                    )
                    outbox[box, h, lines[k + 1] * 2 + core] = jnp.where(
                        left_half, pltpu.roll(upper, 64, 1), lower
                    )

            def send(device):
                pltpu.make_async_remote_copy(
                    src_ref=outbox.at[box, h, device],
                    dst_ref=inbox.at[exchange, h, me],
                    send_sem=send_sem.at[exchange, h, s],
                    recv_sem=recv_sem.at[exchange, h],
                    device_id=(device,),
                    device_id_type=MESH,
                ).start()

            for k in range(group):
                if k > 0:
                    for core in range(2):
                        send(lines[k] * 2 + core)
                else:

                    @pl.when(s > 0)
                    def _():
                        for core in range(2):
                            send(lines[0] * 2 + core)

                    @pl.when(s == 0)
                    def _():
                        send(me + 1 - 2 * lax.rem(me, 2))

            return carry

        lax.fori_loop(0, LINES // group, step, 0)
        inbox[exchange, h, me] = outbox[box, h, me]

    def moved(exchange, h, group, blocks):
        part = inbox.at[exchange, h, pl.ds(0, blocks)]
        return pltpu.make_async_remote_copy(
            src_ref=part,
            dst_ref=part,
            send_sem=send_sem.at[exchange, h, group],
            recv_sem=recv_sem.at[exchange, h],
            device_id=(lax.rem(me + 1, DEVICES),),
            device_id_type=MESH,
        )

    def wait_sent(exchange, h, first, last):
        for group in range(first, last):
            moved(exchange, h, group, 16 if group else 15).wait_send()

    def wait_arrived(exchange, h):
        moved(exchange, h, 0, DEVICES - 1).wait_recv()

    def arrived(exchange, h, y):
        zero, one = inbox[exchange, h, 2 * y], inbox[exchange, h, 2 * y + 1]
        return jnp.concatenate(
            [
                jnp.where(left_half, zero, pltpu.roll(one, 64, 1)),
                jnp.where(left_half, pltpu.roll(zero, 64, 1), one),
            ],
            axis=0,
        )

    def stage_zero(h):
        wait_load(held_c, load_sem.at[0, h], h)
        first_half(held_c.at[h], h)

        def write(y, value):
            held_w[h, rows_of(y), :] = value

        combined(inner, h, write)
        if h == 0:
            pl.semaphore_wait(barrier, DEVICES - 1)
        post(0, h, held_w.at[h])

    def stage_one(h):
        wait_load(held_g, load_sem.at[1, h], h)

        def start(g, carry):
            rows = pl.ds(pl.multiple_of(g * 512, 512), 512)
            held_g[h, rows, :] = step_size * held_g[h, rows, :] + held_w[h, rows, :]
            return carry

        lax.fori_loop(0, SLAB // 512, start, 0)
        first_half(held_g.at[h], h)

        def write(y, value):
            held_p[h, rows_of(y), :] = value

        combined(inner, h, write)
        if h == 0:
            post(1, h, held_p.at[h])

    def stage_two(h):
        wait_sent(0, h, 0, 8)
        wait_arrived(0, h)

        def gather(y, carry):
            rows = rows_of(y)
            value = arrived(0, h, y)
            held_w[h, rows, :] = value
            held_c[h, rows, :] = held_c[h, rows, :] + held_g[h, rows, :] + value
            return carry

        lax.fori_loop(0, LINES, gather, 0, unroll=8)
        first_half(held_w.at[h], h)

        def write(y, value):
            rows = rows_of(y)
            held_g[h, rows, :] = (
                (1.0 / 6.0) * value
                + (1.0 / 24.0) * held_p[h, rows, :]
                + (1.0 / 3.0) * held_w[h, rows, :]
            )

        combined(inner, h, write)

    def stage_three(h):
        wait_arrived(1, h)
        wait_sent(1, h, AHEAD_ONE if h == 0 else AHEAD_TWO, 8)

        def gather(y, carry):
            rows = rows_of(y)
            value = arrived(1, h, y)
            held_g[h, rows, :] = held_g[h, rows, :] + 0.125 * value
            held_w[h, rows, :] = 0.5 * held_w[h, rows, :] + (1.0 / 6.0) * (
                held_p[h, rows, :] + value
            )
            return carry

        lax.fori_loop(0, LINES, gather, 0, unroll=8)
        first_half(held_g.at[h], h)

        def write_one(y, value):
            rows = rows_of(y)
            held_w[h, rows, :] = held_w[h, rows, :] + value

        combined(inner, h, write_one)
        first_half(held_w.at[h], h)

        def write_two(y, value):
            rows = rows_of(y)
            total = value + 0.5 * held_p[h, rows, :]
            outer[rows, :] = total
            held_c[h, rows, :] = held_c[h, rows, :] + total

        combined(inner, h, write_two)
        if h == 0:
            wait_sent(1, 1, 0, AHEAD_TWO)
        post(2, h, outer)

    def stage_last(h):
        wait_arrived(2, h)
        wait_sent(2, h, 0, 8)

        def group(g, carry):
            for k in range(8):
                rows = rows_of(g * 8 + k)
                held_g[h, rows, :] = held_c[h, rows, :] + arrived(2, h, g * 8 + k)
            for k in range(8):
                y = g * 8 + k
                pltpu.make_async_copy(
                    held_g.at[h, rows_of(y), :],
                    advanced.at[h, :, pl.ds(pl.multiple_of(y * WIDTH, WIDTH), WIDTH)],
                    store_sem.at[h],
                ).start()
            return carry

        lax.fori_loop(0, LINES // 8, group, 0)

    prepare(0)
    stage_zero(0)
    prepare(1)
    load(covariance, held_c, load_sem.at[0, 1], 1)
    for h in range(2):
        load(forcing, held_g, load_sem.at[1, h], h)
    stage_zero(1)
    for stage in (stage_one, stage_two):
        for h in range(2):
            stage(h)
    wait_sent(1, 0, 0, AHEAD_ONE)
    post(1, 1, held_p.at[1])
    for stage in (stage_three, stage_last):
        for h in range(2):
            stage(h)
    for h in range(2):
        wait_load(held_g, store_sem.at[h], h)


def on_device(covariance, forcing, coefficient, y_operator, z_operator):
    slab = pltpu.VMEM((2, SLAB, WIDTH), jnp.float32)
    part = pltpu.VMEM((SLAB, WIDTH), jnp.float32)
    hbm = pl.BlockSpec(memory_space=pl.ANY)
    vmem = pl.BlockSpec(memory_space=pltpu.VMEM)
    return pl.pallas_call(
        kernel,
        out_shape=jax.ShapeDtypeStruct(covariance.shape, jnp.float32),
        in_specs=[hbm, hbm, vmem, vmem, vmem],
        out_specs=hbm,
        scratch_shapes=[
            slab, slab, slab, slab, part, part, part,
            pltpu.VMEM((2, 2, DEVICES, 32, WIDTH), jnp.float32),
            pltpu.VMEM((3, 2, DEVICES, 32, WIDTH), jnp.float32),
            pltpu.VMEM((2, LINES, 256), jnp.bfloat16),
            pltpu.VMEM((2, 256, 256), jnp.bfloat16),
            pltpu.SemaphoreType.DMA((2, 2)),
            pltpu.SemaphoreType.DMA((2,)),
            pltpu.SemaphoreType.DMA((3, 2, 8)),
            pltpu.SemaphoreType.DMA((3, 2)),
        ],
        compiler_params=pltpu.CompilerParams(
            collective_id=0, has_side_effects=True, vmem_limit_bytes=56 * 2**20
        ),
        cost_estimate=pl.CostEstimate(
            flops=25 * 10**9, bytes_accessed=12 * 2**20, transcendentals=0
        ),
    )(covariance, forcing, coefficient, y_operator, z_operator)


def solution(mesh):
    placed = (P(None, "col", None), P(None, "col", None), P(), P(), P())
    return jax.shard_map(
        on_device, mesh=mesh, in_specs=placed, out_specs=P(None, "col", None), check_vma=False
    )
```
